256 devices in a mesh: dp: 16 (over z, core), seq: 16 (over x, y).
Axes of the slice: x: 4, y: 4, z: 8, core: 2. Of those that a mesh axis runs over, the one named last changes fastest.
Arguments:
- queries: bfloat16 [16, 2048, 4096], P('dp', 'seq'), may hold values from -16 to 16
- keys: bfloat16 [16, 2048, 512], P('dp', 'seq'), may hold values from -16 to 16
- values: bfloat16 [16, 2048, 512], P('dp', 'seq'), may hold values from -6 to 6
- segment_ids: int32 [4, 2048], P(None, 'seq'), may hold values from 0 to 5, as said below
- rewards: float32 [4, 2048], P(None, 'seq'), may hold values from -6 to 6
- value_weight: bfloat16 [4, 4096], replicated, may hold values from -0.09375 to 0.09375
- subset: int32 [4, 2], replicated, may hold values from 0 to 3, all different within a row
Outputs:
- query_grad: bfloat16 [16, 2048, 4096], P('dp', 'seq')
- key_grad: bfloat16 [16, 2048, 512], P('dp', 'seq')
- value_grad: bfloat16 [16, 2048, 512], P('dp', 'seq')
- td_error: float32 [16, 2048], P('dp', 'seq')
- head_grad: float32 [4, 4096], P(None, 'seq')
The draws below stay inside these ranges and needn't reach their ends.
Inputs may be any that keep to these rules, and one draw needn't show every extreme that they name: `segment_ids`: in each pack, segment ids start at 0 at position 0, never fall, rise by one where a turn starts, and a turn starts only at a multiple of 8; each pack has 6 turns, or 2 where that is fewer.
All inputs are finite; a program needn't handle non-finite values.
Results may differ from the reference program's by a relative error of at most 0.012.
The reference program's roundings to bfloat16 on the way count: a program that leaves them out, or rounds other values in their place, can miss the bound.
Values may be sent and summed in bfloat16 or wider, within the bound.
No kernel may reach another device: no remote copies, remote signals or barrier semaphores. Data moves between devices by JAX's collectives and lax.ppermute only.
A program may use at most 64 MiB of HBM per device.

```python
import jax
import jax.numpy as jnp
from jax import lax

QUERY_HEAD_COUNT = 32
KEY_VALUE_HEADS = 4
HEAD_DIMENSION = 128
SUBSET = 2
MEMBERS = 4
PACK_TOKENS = 2048
BATCHES = 4
MEMBER_PACKS = 16


def draw_queries(key, part):
    key = jax.random.fold_in(key, 3)
    base_offset = jnp.clip(jax.random.normal(key, (MEMBER_PACKS, PACK_TOKENS, QUERY_HEAD_COUNT, HEAD_DIMENSION), jnp.float32), -6.0, 6.0)
    return base_offset.reshape(MEMBER_PACKS, PACK_TOKENS, QUERY_HEAD_COUNT * HEAD_DIMENSION).astype(jnp.bfloat16)


def draw_keys(key, part):
    key = jax.random.fold_in(key, 4)
    base_offset = jnp.clip(jax.random.normal(key, (MEMBER_PACKS, PACK_TOKENS, KEY_VALUE_HEADS, HEAD_DIMENSION), jnp.float32), -6.0, 6.0)
    return base_offset.reshape(MEMBER_PACKS, PACK_TOKENS, KEY_VALUE_HEADS * HEAD_DIMENSION).astype(jnp.bfloat16)


def one_pack(key):
    blocks = PACK_TOKENS // 8
    turn_count = max(2, PACK_TOKENS // 384 + 1)
    order = jax.random.permutation(key, blocks - 1).astype(jnp.int32) + 1
    picked = order[:turn_count - 1]
    starts = jnp.zeros((blocks,), jnp.int32).at[picked].set(1)
    block_ids = jnp.cumsum(starts).astype(jnp.int32)
    return jnp.repeat(block_ids, 8).astype(jnp.int32)


def draw_segment_ids(key, part):
    key = jax.random.fold_in(key, 5)
    pack_keys = jax.random.split(key, BATCHES)
    return jax.vmap(one_pack)(pack_keys).astype(jnp.int32)


def block_levels(rng, extent, pieces, least, top_value):
    def one(dim, blocks):
        heights = jax.random.uniform(jax.random.fold_in(jax.random.fold_in(rng, 6), dim), (blocks,), jnp.float32, least / len(pieces), top_value / len(pieces))
        return jnp.repeat(jnp.exp(heights), extent[dim] // blocks).reshape((-1,) + (1,) * (len(extent) - dim - 1))

    level = one(*pieces[0])
    for cut in pieces[1:]:
        level = level * one(*cut)
    return level


def different_ones(key, rows, number_of, top, lift):
    order = jax.random.permutation(jax.random.fold_in(key, 1), number_of)
    pull = order
    for power in range(3):
        pull = pull * pull // number_of
    pull = pull * lift // number_of
    lots = jax.random.randint(jax.random.fold_in(key, 2), (rows, number_of), 0, 4096) + pull
    fixed_rows = jax.random.permutation(jax.random.fold_in(key, 3), rows)[jnp.arange(number_of) % rows]
    lots = jnp.where(jnp.arange(rows)[:, None] == fixed_rows[None, :], 1 << 14, lots)
    merit = lots * number_of + jnp.arange(number_of)
    return lax.top_k(merit.astype(jnp.int32), top)[1].astype(jnp.int32)


def gaussian(key, shape, spread, limit, cuts=(), kind=jnp.bfloat16):
    drawn = jax.random.normal(key, shape, jnp.float32) * spread
    if len(cuts) > 0:
        drawn = block_levels(key, shape, cuts, -0.22, 0.18) * drawn
    return jnp.clip(drawn, min=-limit, max=limit).astype(kind)


def setup_inputs(seed: int = 0) -> dict:
    key_list = jax.random.split(jax.random.key(seed), 8)
    queries = draw_queries(jax.random.fold_in(key_list[7], 71), 0)
    keys = draw_keys(jax.random.fold_in(key_list[7], 71), 0)
    values = gaussian(key_list[2], (MEMBER_PACKS, PACK_TOKENS, KEY_VALUE_HEADS * HEAD_DIMENSION), 1.0, 6.0, ((0, 16), (1, 16)))
    segment_ids = draw_segment_ids(jax.random.fold_in(key_list[7], 71), 0)
    rewards = gaussian(key_list[4], (BATCHES, PACK_TOKENS), 1.0, 6.0, ((1, 16),), jnp.float32)
    value_weight = gaussian(key_list[5], (MEMBERS, QUERY_HEAD_COUNT * HEAD_DIMENSION), (QUERY_HEAD_COUNT * HEAD_DIMENSION) ** -0.5, 0.09375)
    subset = different_ones(key_list[6], MEMBERS, MEMBERS, SUBSET, 0)
    return dict(queries=queries, keys=keys, values=values, segment_ids=segment_ids, rewards=rewards, value_weight=value_weight, subset=subset)


discount = 0.99


def visible_mask(segment_ids, first_row, row_count):
    grand_total = segment_ids.shape[0]
    query_pos = first_row + jnp.arange(row_count, dtype=jnp.int32)
    key_pos = jnp.arange(grand_total, dtype=jnp.int32)
    query_seg = lax.dynamic_slice_in_dim(segment_ids, first_row, row_count, 0)
    return (key_pos[None, :] <= query_pos[:, None]) & (query_seg[:, None] == segment_ids[None, :])


def attend_prob(query_rows, key_rows, visible):
    scores = jnp.einsum('qgd,kd->gqk', query_rows.astype(jnp.float32), key_rows.astype(jnp.float32)) * (HEAD_DIMENSION ** -0.5)
    scores = jnp.where(visible[None], scores, -jnp.inf)
    row_max = jnp.max(scores, axis=-1, keepdims=True)
    exponent = jnp.exp(scores - row_max)
    return exponent / jnp.sum(exponent, axis=-1, keepdims=True)


def forward_head(queries, key_rows, value_rows, segment_ids):
    grand_total = queries.shape[0]
    span = min(512, grand_total)
    count = grand_total // span

    def one_block(block):
        first_row = (block * span).astype(jnp.int32)
        query_rows = lax.dynamic_slice_in_dim(queries, first_row, span, 0)
        weights = attend_prob(query_rows, key_rows, visible_mask(segment_ids, first_row, span))
        weights_b = lax.optimization_barrier(weights.astype(jnp.bfloat16)).astype(jnp.float32)
        output = jnp.einsum('gqk,kd->qgd', weights_b, value_rows.astype(jnp.float32))
        return output.astype(jnp.bfloat16)

    blocks = lax.map(one_block, jnp.arange(count, dtype=jnp.int32))
    return blocks.reshape(queries.shape)


def backward_head(queries, key_rows, value_rows, segment_ids, attended, cotangent):
    grand_total = queries.shape[0]
    span = min(512, grand_total)
    count = grand_total // span
    zeros_acc = jnp.zeros((grand_total, key_rows.shape[1]), jnp.float32)

    def step(carry, block):
        key_acc, value_acc = carry
        first_row = (block * span).astype(jnp.int32)
        query_rows = lax.dynamic_slice_in_dim(queries, first_row, span, 0)
        out_rows = lax.dynamic_slice_in_dim(attended, first_row, span, 0)
        grad_rows = lax.dynamic_slice_in_dim(cotangent, first_row, span, 0).astype(jnp.float32)
        weights = attend_prob(query_rows, key_rows, visible_mask(segment_ids, first_row, span))
        weights_b = lax.optimization_barrier(weights.astype(jnp.bfloat16)).astype(jnp.float32)
        value_acc = value_acc + jnp.einsum('gqk,qgd->kd', weights_b, grad_rows)
        dprob = jnp.einsum('qgd,kd->gqk', grad_rows, value_rows.astype(jnp.float32))
        delta = jnp.sum(grad_rows * out_rows.astype(jnp.float32), axis=-1).T
        dscore = (weights * (dprob - delta[:, :, None]) * (HEAD_DIMENSION ** -0.5)).astype(jnp.bfloat16)
        dscore_f = lax.optimization_barrier(dscore).astype(jnp.float32)
        query_portion = jnp.einsum('gqk,kd->qgd', dscore_f, key_rows.astype(jnp.float32)).astype(jnp.bfloat16)
        key_acc = key_acc + jnp.einsum('gqk,qgd->kd', dscore_f, query_rows.astype(jnp.float32))
        return (key_acc, value_acc), query_portion

    (key_acc, value_acc), parts = lax.scan(step, (zeros_acc, zeros_acc), jnp.arange(count, dtype=jnp.int32))
    return parts.reshape(queries.shape), key_acc, value_acc


def reference(queries, keys, values, segment_ids, rewards, value_weight, subset):
    pairs = queries.shape[0]
    grand_total = queries.shape[1]
    batches = pairs // MEMBERS
    head_group = QUERY_HEAD_COUNT // KEY_VALUE_HEADS
    seg_pairs = jnp.repeat(segment_ids, MEMBERS, axis=0)
    reward_pairs = jnp.repeat(rewards, MEMBERS, axis=0)
    weight_pairs = jnp.tile(value_weight, (batches, 1))

    def heads_view(member_queries, member_keys, member_value_rows):
        return (member_queries.reshape(grand_total, KEY_VALUE_HEADS, head_group, HEAD_DIMENSION), member_keys.reshape(grand_total, KEY_VALUE_HEADS, HEAD_DIMENSION),
                member_value_rows.reshape(grand_total, KEY_VALUE_HEADS, HEAD_DIMENSION))

    forward_all = jax.vmap(forward_head, in_axes=(1, 1, 1, None), out_axes=1)

    def member_forward(array_list):
        q_head, k_head, v_head = heads_view(array_list[0], array_list[1], array_list[2])
        return forward_all(q_head, k_head, v_head, array_list[3]).reshape(grand_total, QUERY_HEAD_COUNT * HEAD_DIMENSION)

    attended = lax.map(member_forward, (queries, keys, values, seg_pairs))
    estimates = jnp.einsum('mtc,mc->mt', attended.astype(jnp.float32), weight_pairs.astype(jnp.float32),
                           precision=lax.Precision.HIGHEST)
    ahead_values = jnp.concatenate([estimates[:, 1:], jnp.zeros((pairs, 1), jnp.float32)], axis=1)
    base_rows = (jnp.arange(pairs, dtype=jnp.int32) // MEMBERS) * MEMBERS
    row_index = (base_rows[:, None] + jnp.tile(subset, (batches, 1))).astype(jnp.int32)
    picked = ahead_values[row_index]
    lowest_next = jnp.min(picked, axis=1)
    continuing = jnp.concatenate([seg_pairs[:, 1:] == seg_pairs[:, :-1], jnp.zeros((pairs, 1), dtype=bool)], axis=1)
    lowest = jnp.where(continuing, lowest_next, jnp.zeros_like(lowest_next))
    td_error = estimates - (reward_pairs + discount * lowest)
    pair_grad = jnp.einsum('mtc,mt->mc', attended.astype(jnp.float32), td_error, precision=lax.Precision.HIGHEST)
    head_grad = jnp.sum(pair_grad.reshape(batches, MEMBERS, QUERY_HEAD_COUNT * HEAD_DIMENSION), axis=0)
    cotangent = (td_error[:, :, None] * weight_pairs.astype(jnp.float32)[:, None, :]).astype(jnp.bfloat16)
    backward_all = jax.vmap(backward_head, in_axes=(1, 1, 1, None, 1, 1), out_axes=(1, 1, 1))

    def member_backward(array_list):
        q_head, k_head, v_head = heads_view(array_list[0], array_list[1], array_list[2])
        head_output = array_list[4].reshape(grand_total, KEY_VALUE_HEADS, head_group, HEAD_DIMENSION)
        head_gradient = array_list[5].reshape(grand_total, KEY_VALUE_HEADS, head_group, HEAD_DIMENSION)
        query_portion, key_portion, value_portion = backward_all(q_head, k_head, v_head, array_list[3], head_output, head_gradient)
        return (query_portion.reshape(grand_total, QUERY_HEAD_COUNT * HEAD_DIMENSION), key_portion.reshape(grand_total, KEY_VALUE_HEADS * HEAD_DIMENSION).astype(jnp.bfloat16),
                value_portion.reshape(grand_total, KEY_VALUE_HEADS * HEAD_DIMENSION).astype(jnp.bfloat16))

    query_grad, key_grad, value_grad = lax.map(member_backward,
                                               (queries, keys, values, seg_pairs, attended, cotangent))
    return query_grad, key_grad, value_grad, td_error, head_grad
```

```python
import functools

import jax
import jax.numpy as jnp
from jax import lax
from jax.experimental import pallas as pl
from jax.experimental.pallas import tpu as pltpu
from jax.sharding import PartitionSpec as P

HEAD = 128
MEMBERS = 4
SIDE = 4
CHUNKS = SIDE * SIDE
GROUP = 8
WIDE = GROUP * HEAD
TURNS = 6
DISCOUNT = 0.99
SCALE = HEAD**-0.5
LOG2E = 1.4426950408889634
AUX = 32
GRAD_ROWS = HEAD + 2 * GROUP
F32 = jnp.float32
BF16 = jnp.bfloat16
NT = (((1,), (1,)), ((), ()))
TN = (((0,), (0,)), ((), ()))


def dot(lhs, rhs, dims=(((1,), (0,)), ((), ()))):
    return lax.dot_general(lhs, rhs, dims, preferred_element_type=F32)


def place():
    seq = lax.axis_index("seq")
    return lax.div(seq, SIDE), lax.rem(seq, SIDE)


def ahead_by(index, steps):
    return lax.rem(index + (steps + SIDE), SIDE)


def along_x(value, steps):
    pairs = [(i, (i // SIDE + steps) % SIDE * SIDE + i % SIDE) for i in range(CHUNKS)]
    return lax.ppermute(value, "seq", pairs)


def along_y(value, steps):
    pairs = [(i, i // SIDE * SIDE + (i % SIDE + steps) % SIDE) for i in range(CHUNKS)]
    return lax.ppermute(value, "seq", pairs)


def split_two(value):
    high = value.astype(BF16).astype(F32)
    return high, value - high


def group_weights(weight_ref, member, group):
    rows = weight_ref[:, pl.ds(pl.multiple_of(group * WIDE, WIDE), WIDE)].astype(F32)
    mine = lax.broadcasted_iota(jnp.int32, rows.shape, 0) == member
    row = jnp.sum(jnp.where(mine, rows, 0.0), axis=0, keepdims=True)
    return jnp.concatenate([row[:, h * HEAD : (h + 1) * HEAD] for h in range(GROUP)], axis=0)


def prepare_kernel(key_ref, value_ref, seg_ref, reward_ref, weight_ref, *outs):
    a, _ = place()
    dp = lax.axis_index("dp")
    member, pack = lax.rem(dp, MEMBERS), lax.div(dp, MEMBERS)
    mine = lax.broadcasted_iota(jnp.int32, seg_ref.shape, 0) == pack
    seg = jnp.sum(jnp.where(mine, seg_ref[...].astype(F32), 0.0), axis=0, keepdims=True)
    reward = jnp.sum(jnp.where(mine, reward_ref[...], 0.0), axis=0, keepdims=True)
    first, rest = split_two(reward)
    second, third = split_two(rest)
    tail = jnp.zeros((AUX - 2 * GROUP - 4, HEAD), F32)
    for s in range(SIDE):
        group = ahead_by(a, s)
        columns = pl.ds(pl.multiple_of(group * HEAD, HEAD), HEAD)
        weights = group_weights(weight_ref, member, group).astype(BF16)
        u = dot(weights, value_ref[0, :, columns], NT)
        high, low = split_two(u)
        outs[s][:HEAD, :] = key_ref[0, :, columns]
        aux = jnp.concatenate([high, low, seg, first, second, third, tail], axis=0)
        outs[s][HEAD:, :] = aux.astype(BF16)
        outs[SIDE + s][...] = value_ref[0, :, columns]


def selector(rows):
    row = lax.broadcasted_iota(jnp.int32, (rows, WIDE), 0)
    head = lax.broadcasted_iota(jnp.int32, (rows, WIDE), 1) // HEAD
    return jnp.where(row % GROUP == head, 1.0, 0.0).astype(BF16)


def load_queries(parts, stacked):
    for s in range(SIDE):
        for h in range(GROUP):
            stacked[s, h * HEAD : (h + 1) * HEAD, :] = parts[s][:, h * HEAD : (h + 1) * HEAD]


def load_keys(parts, keys, us, a, b):
    for t in range(SIDE):
        for s in range(SIDE):
            chunk = ahead_by(a, -s) * SIDE + ahead_by(b, -t)
            keys[pl.ds(chunk, 1)] = parts[t][s : s + 1, :HEAD, :]
            us[pl.ds(chunk, 1)] = parts[t][s : s + 1, HEAD : HEAD + 2 * GROUP, :]


def turn_starts(parts):
    row = HEAD + 2 * GROUP
    segs = jnp.concatenate(
        [parts[t][s, row : row + 16, :].astype(F32)[:1] for t in range(SIDE) for s in range(SIDE)], axis=0
    )
    return [jnp.sum(jnp.where(segs < turn, 1.0, 0.0)).astype(jnp.int32) for turn in range(1, TURNS)]


def latest(starts, position):
    out = jnp.zeros_like(position)
    for start in starts:
        out = jnp.maximum(out, jnp.where(start <= position, start, 0))
    return out


def heads_of(value):
    return [value[:, h * HEAD : (h + 1) * HEAD] for h in range(value.shape[1] // HEAD)]


def visible_at(block, row_pos, row_start):
    key_pos = block * HEAD + lax.broadcasted_iota(jnp.int32, (HEAD, HEAD), 0)
    return (key_pos >= row_start) & (key_pos <= row_pos)


def forward_kernel(*refs):
    q_parts, k_parts, refs = refs[:4], refs[4:8], refs[8:]
    g_outs, (est_ref, max_ref, inv_ref, e_ref, start_ref), refs = refs[:4], refs[4:9], refs[9:]
    stacked, keys, us, scores, grad, whole = refs
    a, b = place()
    load_queries(q_parts, stacked)
    load_keys(k_parts, keys, us, a, b)
    starts = turn_starts(k_parts)
    for i, start in enumerate(starts):
        start_ref[i] = start
    est_ref[...] = jnp.zeros_like(est_ref)
    pick = selector(2 * GROUP)
    lanes = lax.broadcasted_iota(jnp.int32, (1, HEAD), 1)

    def one_chunk(s, _):
        row = lax.rem(a - s + SIDE, SIDE)
        chunk = row * SIDE + b
        row_pos = chunk * HEAD + lanes
        row_start = latest(starts, row_pos)
        low = lax.div(latest(starts, chunk * HEAD), HEAD)
        queries = stacked[s]

        def first(block, top):
            score = dot(keys[block], queries, NT)
            seen = visible_at(block, row_pos, row_start)
            score = jnp.concatenate([jnp.where(seen, x, -1e30) for x in heads_of(score)], axis=1)
            scores[block] = score
            return jnp.maximum(top, jnp.max(score.reshape(HEAD // 8, 8, WIDE), axis=0))

        top = lax.fori_loop(low, chunk + 1, first, jnp.full((8, WIDE), -1e30, F32))
        top = jnp.max(top, axis=0, keepdims=True)

        def second(block, carry):
            total, weighted = carry
            prob = jnp.exp2((scores[block] - top) * (SCALE * LOG2E))
            scores[block] = prob
            u = dot(us[block], pick, TN)
            total = total + jnp.sum(prob.reshape(HEAD // 8, 8, WIDE), axis=0)
            weighted = weighted + jnp.sum((prob * u).reshape(HEAD // 8, 8, WIDE), axis=0)
            return total, weighted

        zero = jnp.zeros((8, WIDE), F32)
        total, weighted = lax.fori_loop(low, chunk + 1, second, (zero, zero))
        inverse = 1.0 / jnp.sum(total, axis=0, keepdims=True)
        e = jnp.sum(weighted, axis=0, keepdims=True) * inverse
        grad[...] = jnp.zeros_like(grad)

        def third(block, _):
            u = dot(us[block], pick, TN)
            change = (scores[block] * (u - e)).astype(BF16)
            grad[...] += dot(keys[block], change, TN)
            return 0

        lax.fori_loop(low, chunk + 1, third, 0)
        est = functools.reduce(jnp.add, heads_of(e))
        est_ref[pl.ds(row, 1), :] = est
        max_ref[pl.ds(s, 1), :] = top
        inv_ref[pl.ds(s, 1), :] = inverse
        e_ref[pl.ds(s, 1), :] = e
        out = grad[...] * (inverse * SCALE)
        whole[s] = jnp.concatenate([x.T for x in heads_of(out)], axis=1).astype(BF16)
        return 0

    lax.fori_loop(0, SIDE, one_chunk, 0)
    for s in range(SIDE):
        g_outs[s][...] = whole[s]


def td_rows(own, others, rewards, starts, subset_ref, b, member):
    shape = (8, HEAD)
    rows = lax.broadcasted_iota(jnp.int32, shape, 0)
    lanes = lax.broadcasted_iota(jnp.int32, shape, 1)
    position = (rows * SIDE + b) * HEAD + lanes
    ahead = []
    for table, after in others:
        after = jnp.where(b == SIDE - 1, pltpu.roll(after, 7, 0), after)
        ahead.append(jnp.where(lanes == HEAD - 1, pltpu.roll(after, HEAD - 1, 1), pltpu.roll(table, HEAD - 1, 1)))
    lowest = None
    for k in range(subset_ref.shape[1]):
        apart = jnp.bitwise_xor(subset_ref[member, k], member)
        chosen = ahead[0]
        for i in range(1, MEMBERS):
            chosen = jnp.where(apart == i, ahead[i], chosen)
        lowest = chosen if lowest is None else jnp.minimum(lowest, chosen)
    goes_on = position + 1 < CHUNKS * HEAD
    for start in starts:
        goes_on = goes_on & (position + 1 != start)
    lowest = jnp.where(goes_on, lowest, 0.0)
    return own - (rewards + DISCOUNT * lowest)


def backward_kernel(*refs):
    q_parts, k_parts, v_parts, refs = refs[:4], refs[4:8], refs[8:12], refs[12:]
    (max_ref, inv_ref, e_ref, start_ref, subset_ref, e0, e1, n0, n1, far), refs = refs[:10], refs[10:]
    (td_out, *d_outs), refs = refs[:5], refs[5:]
    h_outs, refs = refs[:4], refs[4:]
    stacked, keys, us, key_grad, sums, rewards, tds = refs
    a, b = place()
    member = lax.rem(lax.axis_index("dp"), MEMBERS)
    load_queries(q_parts, stacked)
    load_keys(k_parts, keys, us, a, b)
    starts = [start_ref[i] for i in range(TURNS - 1)]
    row = HEAD + 2 * GROUP
    rewards[...] = jnp.zeros_like(rewards)
    for s in range(SIDE):
        part = k_parts[0][s, row : row + 16, :].astype(F32)
        rewards[pl.ds(ahead_by(a, -s), 1), :] = part[1:2] + (part[2:3] + part[3:4])
    others = [(e0[...], n0[...]), (e1[...], n1[...]), (far[0:8], far[16:24]), (far[8:16], far[24:32])]
    tds[...] = td_rows(e0[...], others, rewards[...], starts, subset_ref, b, member)
    td_out[...] = tds[pl.ds(a, 1), :]
    key_grad[...] = jnp.zeros_like(key_grad)
    sums[...] = jnp.zeros_like(sums)
    pick = selector(2 * GROUP)
    pick_sum = selector(GROUP)
    lanes = lax.broadcasted_iota(jnp.int32, (1, HEAD), 1)

    def one_chunk(s, _):
        row = lax.rem(a - s + SIDE, SIDE)
        chunk = row * SIDE + b
        row_pos = chunk * HEAD + lanes
        row_start = latest(starts, row_pos)
        low = lax.div(latest(starts, chunk * HEAD), HEAD)
        queries = stacked[s]
        top = max_ref[pl.ds(s, 1), :]
        e = e_ref[pl.ds(s, 1), :]
        td = jnp.concatenate([tds[pl.ds(row, 1), :]] * GROUP, axis=1) * inv_ref[pl.ds(s, 1), :]

        def one_block(block, _):
            score = dot(keys[block], queries, NT)
            seen = visible_at(block, row_pos, row_start)
            prob = jnp.exp2((score - top) * (SCALE * LOG2E)) * td
            prob = jnp.concatenate([jnp.where(seen, x, 0.0) for x in heads_of(prob)], axis=1)
            u = dot(us[block], pick, TN)
            sums[block] += dot(pick_sum, prob.astype(BF16), NT)
            key_grad[block] += dot((prob * (u - e)).astype(BF16), queries)
            return 0

        return lax.fori_loop(low, chunk + 1, one_block, 0)

    lax.fori_loop(0, SIDE, one_chunk, 0)
    heads = jnp.zeros((GROUP, HEAD), F32)
    for t in range(SIDE):
        for s in range(SIDE):
            chunk = ahead_by(a, -s) * SIDE + ahead_by(b, -t)
            high, low = split_two(sums[pl.ds(chunk, 1)][0])
            value = v_parts[t][s]
            heads = heads + (dot(high.astype(BF16), value) + dot(low.astype(BF16), value))
            out = d_outs[(SIDE - t) % SIDE]
            base = s * GRAD_ROWS
            out[base : base + HEAD, :] = (key_grad[pl.ds(chunk, 1)][0] * SCALE).astype(BF16)
            out[base + HEAD : base + GRAD_ROWS, :] = jnp.concatenate([high, low], axis=0).astype(BF16)
    for t in range(SIDE):
        first = 2 * ahead_by(b, t)
        h_outs[t][...] = pltpu.roll(heads, lax.rem(GROUP - first, GROUP), 0)


def collect_kernel(d0, d1, d2, d3, *outs):
    for s in range(SIDE):
        base = s * GRAD_ROWS
        keys = [d[base : base + HEAD, :].astype(F32) for d in (d0, d1, d2, d3)]
        sums = [d[base + HEAD : base + GRAD_ROWS, :].astype(F32) for d in (d0, d1, d2, d3)]
        total = functools.reduce(jnp.add, [x[:GROUP] + x[GROUP:] for x in sums])
        outs[s][:HEAD, :] = functools.reduce(jnp.add, keys).astype(BF16)
        outs[s][HEAD:, :] = jnp.concatenate(split_two(total), axis=0).astype(BF16)


def finish_queries_kernel(td_ref, g0, g1, g2, g3, out):
    a, _ = place()
    td = jnp.broadcast_to(td_ref[...], (HEAD, HEAD)).T
    for s, part in enumerate((g0, g1, g2, g3)):
        base = ahead_by(a, s) * WIDE
        for h in range(GROUP):
            columns = pl.ds(pl.multiple_of(base + h * HEAD, HEAD), HEAD)
            block = part[:, h * HEAD : (h + 1) * HEAD].astype(F32)
            out[0, :, columns] = (block * td).astype(BF16)


def finish_keys_kernel(weight_ref, r0, r1, r2, r3, key_out, value_out):
    a, _ = place()
    member = lax.rem(lax.axis_index("dp"), MEMBERS)
    for s, part in enumerate((r0, r1, r2, r3)):
        group = ahead_by(a, s)
        columns = pl.ds(pl.multiple_of(group * HEAD, HEAD), HEAD)
        weights = group_weights(weight_ref, member, group)
        weights = jnp.concatenate([weights, weights], axis=0).astype(BF16)
        key_out[0, :, columns] = part[:HEAD, :]
        value_out[0, :, columns] = dot(part[HEAD:, :], weights, TN).astype(BF16)


def finish_heads_kernel(h0, h1, h2, h3, out):
    member = lax.rem(lax.axis_index("dp"), MEMBERS)
    rows = lax.broadcasted_iota(jnp.int32, (MEMBERS, HEAD), 0)
    for j in range(2):
        total = jnp.zeros((MEMBERS, HEAD), F32)
        for i, part in enumerate((h0, h1, h2, h3)):
            total = jnp.where(rows == jnp.bitwise_xor(member, i), part[j : j + 1, :], total)
        out[:, j * HEAD : (j + 1) * HEAD] = total


def call(kernel, outs, operands, scratch=(), in_smem=(), out_smem=(), limit=None, cost=None):
    def spec(i, smem):
        return pl.BlockSpec(memory_space=pltpu.SMEM if i in smem else pltpu.VMEM)

    return pl.pallas_call(
        kernel,
        out_shape=[jax.ShapeDtypeStruct(s, t) for s, t in outs],
        in_specs=[spec(i, in_smem) for i in range(len(operands))],
        out_specs=[spec(i, out_smem) for i in range(len(outs))],
        scratch_shapes=list(scratch),
        compiler_params=pltpu.CompilerParams(vmem_limit_bytes=limit),
        cost_estimate=cost,
    )(*operands)


def per_device(queries, keys, values, segment_ids, rewards, value_weight, subset):
    tok = keys.shape[1]
    a, _ = place()
    prepared = call(
        prepare_kernel,
        [((tok + AUX, HEAD), BF16)] * SIDE + [((tok, HEAD), BF16)] * SIDE,
        (keys, values, segment_ids, rewards, value_weight),
    )
    key_msgs, value_msgs = prepared[:SIDE], prepared[SIDE:]
    q_own = [
        lax.dynamic_slice_in_dim(queries[0], ahead_by(a, s) * WIDE, WIDE, axis=1) for s in range(SIDE)
    ]
    key_rows = jnp.stack([key_msgs[0]] + [along_x(key_msgs[s], s) for s in range(1, SIDE)])
    q_parts = [q_own[0]] + [along_x(q_own[s], s) for s in range(1, SIDE)]
    k_parts = [key_rows] + [along_y(key_rows, t) for t in range(1, SIDE)]
    value_rows = jnp.stack([value_msgs[0]] + [along_x(value_msgs[s], s) for s in range(1, SIDE)])
    v_parts = [value_rows] + [along_y(value_rows, t) for t in range(1, SIDE)]
    stats = (SIDE, WIDE)
    forward = call(
        forward_kernel,
        [((tok, WIDE), BF16)] * SIDE + [((8, HEAD), F32)] + [(stats, F32)] * 3 + [((8,), jnp.int32)],
        (*q_parts, *k_parts),
        [
            pltpu.VMEM((SIDE, WIDE, HEAD), BF16),
            pltpu.VMEM((CHUNKS, HEAD, HEAD), BF16),
            pltpu.VMEM((CHUNKS, 2 * GROUP, HEAD), BF16),
            pltpu.VMEM((CHUNKS, HEAD, WIDE), F32),
            pltpu.VMEM((HEAD, WIDE), F32),
            pltpu.VMEM((SIDE, tok, WIDE), BF16),
        ],
        out_smem=(8,),
        limit=40 * 2**20,
    )
    g_own, (partial, top, inverse, e, starts) = forward[:SIDE], forward[SIDE:]
    g_parts = [g_own[0]] + [along_x(g_own[s], -s) for s in range(1, SIDE)]
    half = partial + lax.ppermute(partial, "seq", [(i, i ^ SIDE) for i in range(CHUNKS)])
    est = half + lax.ppermute(half, "seq", [(i, i ^ 2 * SIDE) for i in range(CHUNKS)])
    dp_count = lax.axis_size("dp")
    partner = {k: [(i, i ^ k) for i in range(dp_count)] for k in (1, 2, 3, 4, 8)}
    est_pair = lax.ppermute(est, "dp", partner[1])
    after = along_y(est, -1)
    both = [
        (i, ((i // CHUNKS) ^ 1) * CHUNKS + i % CHUNKS // SIDE * SIDE + (i - 1) % SIDE)
        for i in range(dp_count * CHUNKS)
    ]
    after_pair = lax.ppermute(est, ("dp", "seq"), both)
    far = lax.ppermute(jnp.concatenate([est, est_pair, after, after_pair]), "dp", partner[2])
    backward = call(
        backward_kernel,
        [((1, tok), F32)] + [((SIDE * GRAD_ROWS, HEAD), BF16)] * SIDE + [((8, HEAD), F32)] * SIDE,
        (*q_parts, *k_parts, *v_parts, top, inverse, e, starts, subset, est, est_pair, after, after_pair, far),
        [
            pltpu.VMEM((SIDE, WIDE, HEAD), BF16),
            pltpu.VMEM((CHUNKS, HEAD, HEAD), BF16),
            pltpu.VMEM((CHUNKS, 2 * GROUP, HEAD), BF16),
            pltpu.VMEM((CHUNKS, HEAD, HEAD), F32),
            pltpu.VMEM((CHUNKS, GROUP, HEAD), F32),
            pltpu.VMEM((8, HEAD), F32),
            pltpu.VMEM((8, HEAD), F32),
        ],
        in_smem=(15, 16),
        limit=40 * 2**20,
    )
    td_local, d_own, h_own = backward[0], backward[1 : 1 + SIDE], backward[1 + SIDE :]
    head_part = h_own[0] + sum(along_y(h_own[t], t) for t in range(1, SIDE))
    head_part = head_part + lax.ppermute(head_part, "dp", partner[4])
    head_part = head_part + lax.ppermute(head_part, "dp", partner[8])
    head_parts = [head_part] + [lax.ppermute(head_part, "dp", partner[k]) for k in range(1, MEMBERS)]
    d_parts = [d_own[0]] + [along_y(d_own[t], t) for t in range(1, SIDE)]
    r_own = call(collect_kernel, [((GRAD_ROWS, HEAD), BF16)] * SIDE, d_parts)
    r_parts = [r_own[0]] + [along_x(r_own[s], -s) for s in range(1, SIDE)]
    (query_grad,) = call(finish_queries_kernel, [(queries.shape, BF16)], (td_local, *g_parts))
    key_grad, value_grad = call(
        finish_keys_kernel, [(keys.shape, BF16), (values.shape, BF16)], (value_weight, *r_parts)
    )
    (head_grad,) = call(finish_heads_kernel, [((MEMBERS, 2 * HEAD), F32)], head_parts)
    return query_grad, key_grad, value_grad, td_local, head_grad


def solution(mesh):
    return jax.shard_map(
        per_device,
        mesh=mesh,
        in_specs=(
            P("dp", "seq", None),
            P("dp", "seq", None),
            P("dp", "seq", None),
            P(None, "seq"),
            P(None, "seq"),
            P(),
            P(),
        ),
        out_specs=(
            P("dp", "seq", None),
            P("dp", "seq", None),
            P("dp", "seq", None),
            P("dp", "seq"),
            P(None, "seq"),
        ),
        check_vma=False,
    )
```

```python
import functools

import jax
import jax.numpy as jnp
from jax import lax
from jax.experimental import pallas as pl
from jax.experimental.pallas import tpu as pltpu
from jax.sharding import PartitionSpec as P

HEAD = 128
MEMBERS = 4
SIDE = 4
CHUNKS = SIDE * SIDE
GROUP = 8
WIDE = GROUP * HEAD
TURNS = 6
DISCOUNT = 0.99
SCALE = HEAD**-0.5
LOG2E = 1.4426950408889634
AUX = 32
GRAD_ROWS = HEAD + 2 * GROUP
F32 = jnp.float32
BF16 = jnp.bfloat16
NT = (((1,), (1,)), ((), ()))
TN = (((0,), (0,)), ((), ()))


def dot(lhs, rhs, dims=(((1,), (0,)), ((), ()))):
    return lax.dot_general(lhs, rhs, dims, preferred_element_type=F32)


def place():
    seq = lax.axis_index("seq")
    return lax.div(seq, SIDE), lax.rem(seq, SIDE)


def ahead_by(index, steps):
    return lax.rem(index + (steps + SIDE), SIDE)


def along_x(value, steps):
    pairs = [(i, (i // SIDE + steps) % SIDE * SIDE + i % SIDE) for i in range(CHUNKS)]
    return lax.ppermute(value, "seq", pairs)


def along_y(value, steps):
    pairs = [(i, i // SIDE * SIDE + (i % SIDE + steps) % SIDE) for i in range(CHUNKS)]
    return lax.ppermute(value, "seq", pairs)


def split_two(value):
    high = value.astype(BF16).astype(F32)
    return high, value - high


def group_weights(weight_ref, member, group):
    rows = weight_ref[:, pl.ds(pl.multiple_of(group * WIDE, WIDE), WIDE)].astype(F32)
    mine = lax.broadcasted_iota(jnp.int32, rows.shape, 0) == member
    row = jnp.sum(jnp.where(mine, rows, 0.0), axis=0, keepdims=True)
    return jnp.concatenate([row[:, h * HEAD : (h + 1) * HEAD] for h in range(GROUP)], axis=0)


def prepare_kernel(*refs):
    query_ref, *sources = refs[:6]
    key_outs, query_outs, targets, sems = refs[6:10], refs[10:14], refs[14:19], refs[19]
    a, _ = place()
    copies = [pltpu.make_async_copy(x, y, sems.at[i]) for i, (x, y) in enumerate(zip(sources, targets))]
    moves = []
    for s in range(SIDE):
        columns = pl.ds(pl.multiple_of(ahead_by(a, s) * WIDE, WIDE), WIDE)
        moves.append(pltpu.make_async_copy(query_ref.at[0, :, columns], query_outs[s], sems.at[len(copies) + s]))
    for copy in copies + moves:
        copy.start()
    for copy in copies:
        copy.wait()
    key_ref, value_ref, seg_ref, reward_ref, weight_ref = targets
    dp = lax.axis_index("dp")
    member, pack = lax.rem(dp, MEMBERS), lax.div(dp, MEMBERS)
    mine = lax.broadcasted_iota(jnp.int32, seg_ref.shape, 0) == pack
    seg = jnp.sum(jnp.where(mine, seg_ref[...].astype(F32), 0.0), axis=0, keepdims=True)
    reward = jnp.sum(jnp.where(mine, reward_ref[...], 0.0), axis=0, keepdims=True)
    first, rest = split_two(reward)
    second, third = split_two(rest)
    tail = jnp.zeros((AUX - 2 * GROUP - 4, HEAD), F32)
    for s in range(SIDE):
        group = ahead_by(a, s)
        columns = pl.ds(pl.multiple_of(group * HEAD, HEAD), HEAD)
        weights = group_weights(weight_ref, member, group).astype(BF16)
        value = value_ref[0, :, columns]
        high, low = split_two(dot(weights, value, NT))
        key_outs[s][:HEAD, :] = key_ref[0, :, columns]
        aux = jnp.concatenate([high, low, seg, first, second, third, tail], axis=0)
        key_outs[s][HEAD : HEAD + AUX, :] = aux.astype(BF16)
        key_outs[s][HEAD + AUX :, :] = value
    for move in moves:
        move.wait()


def selector(rows):
    row = lax.broadcasted_iota(jnp.int32, (rows, WIDE), 0)
    head = lax.broadcasted_iota(jnp.int32, (rows, WIDE), 1) // HEAD
    return jnp.where(row % GROUP == head, 1.0, 0.0).astype(BF16)


def columns_selector():
    head = lax.broadcasted_iota(jnp.int32, (WIDE, HEAD), 0) // HEAD
    column = lax.broadcasted_iota(jnp.int32, (WIDE, HEAD), 1)
    return jnp.where(column == head, 1.0, 0.0).astype(BF16)


def stack_heads(part, stacked):
    for h in range(GROUP):
        stacked[h * HEAD : (h + 1) * HEAD, :] = part[:, h * HEAD : (h + 1) * HEAD]


def turn_heads(part, turned):
    for h in range(GROUP):
        turned[:, h * HEAD : (h + 1) * HEAD] = part[:, h * HEAD : (h + 1) * HEAD].T


def row_of(a, s):
    return lax.rem(a - s + SIDE, SIDE)


def turn_starts(parts):
    row = HEAD + 2 * GROUP
    segs = jnp.concatenate(
        [parts[t][s, row : row + 16, :].astype(F32)[:1] for t in range(SIDE) for s in range(SIDE)], axis=0
    )
    return [jnp.sum(jnp.where(segs < turn, 1.0, 0.0)).astype(jnp.int32) for turn in range(1, TURNS)]


def latest(starts, position):
    out = jnp.zeros_like(position)
    for start in starts:
        out = jnp.maximum(out, jnp.where(start <= position, start, 0))
    return out


def heads_of(value):
    return [value[:, h * HEAD : (h + 1) * HEAD] for h in range(value.shape[1] // HEAD)]


def visible_at(block, row_pos, row_start, count=1):
    key_pos = block * HEAD + lax.broadcasted_iota(jnp.int32, (count * HEAD, HEAD), 0)
    return (key_pos >= row_start) & (key_pos <= row_pos)


def assemble_kernel(p0, p1, p2, p3, keys, turned, us, wide_u, rewards, start_ref):
    a, b = place()
    parts = (p0, p1, p2, p3)
    pick = selector(2 * GROUP)
    keys[CHUNKS] = jnp.zeros((HEAD, HEAD), BF16)
    turned[:, CHUNKS * HEAD :] = jnp.zeros((HEAD, HEAD), BF16)
    us[CHUNKS] = jnp.zeros((2 * GROUP, HEAD), BF16)
    wide_u[CHUNKS] = jnp.zeros((HEAD, WIDE), F32)
    for t in range(SIDE):
        for s in range(SIDE):
            chunk = ahead_by(a, -s) * SIDE + ahead_by(b, -t)
            keys[pl.ds(chunk, 1)] = parts[t][s : s + 1, :HEAD, :]
            turned[:, pl.ds(pl.multiple_of(chunk * HEAD, HEAD), HEAD)] = parts[t][s, :HEAD, :].T
            u = parts[t][s, HEAD : HEAD + 2 * GROUP, :]
            us[pl.ds(chunk, 1)] = u[None]
            wide_u[pl.ds(chunk, 1)] = dot(u, pick, TN)[None]
    for i, start in enumerate(turn_starts(parts)):
        start_ref[i] = start
    row = HEAD + 2 * GROUP
    rewards[...] = jnp.zeros_like(rewards)
    for s in range(SIDE):
        part = p0[s, row : row + 16, :].astype(F32)
        rewards[pl.ds(ahead_by(a, -s), 1), :] = part[1:2] + (part[2:3] + part[3:4])


def forward_kernel(s, *refs):
    q_part, keys, turned, wide_u, start_ref, est_in, refs = *refs[:6], refs[6:]
    g_out, est_ref, max_ref, inv_ref, e_ref, stacked, scores, grad = refs
    a, b = place()
    turn_heads(q_part, stacked)
    starts = [start_ref[i] for i in range(TURNS - 1)]
    lanes = lax.broadcasted_iota(jnp.int32, (1, HEAD), 1)
    row = row_of(a, s)
    chunk = row * SIDE + b
    row_pos = chunk * HEAD + lanes
    row_start = latest(starts, row_pos)
    low = lax.div(latest(starts, chunk * HEAD), HEAD)

    pairs = lax.div(chunk - low + 2, 2)

    def first(pair, top):
        block = low + 2 * pair
        key = keys[pl.ds(block, 2)].reshape(2 * HEAD, HEAD)
        score = dot(key, stacked[...])
        seen = visible_at(block, row_pos, row_start, 2)
        score = jnp.concatenate([jnp.where(seen, x, -1e30) for x in heads_of(score)], axis=1)
        scores[pl.ds(block, 2)] = score.reshape(2, HEAD, WIDE)
        return jnp.maximum(top, jnp.max(score.reshape(HEAD // 4, 8, WIDE), axis=0))

    top = lax.fori_loop(0, pairs, first, jnp.full((8, WIDE), -1e30, F32))
    top = jnp.max(top, axis=0, keepdims=True)

    def second(pair, carry):
        total, weighted = carry
        block = low + 2 * pair
        prob = jnp.exp2((scores[pl.ds(block, 2)] - top) * (SCALE * LOG2E))
        scores[pl.ds(block, 2)] = prob
        weight = prob * wide_u[pl.ds(block, 2)]
        total = total + jnp.sum(prob.reshape(HEAD // 4, 8, WIDE), axis=0)
        weighted = weighted + jnp.sum(weight.reshape(HEAD // 4, 8, WIDE), axis=0)
        return total, weighted

    zero = jnp.zeros((8, WIDE), F32)
    total, weighted = lax.fori_loop(0, pairs, second, (zero, zero))
    inverse = 1.0 / jnp.sum(total, axis=0, keepdims=True)
    e = jnp.sum(weighted, axis=0, keepdims=True) * inverse
    grad[...] = jnp.zeros_like(grad)

    def third(pair, _):
        block = low + 2 * pair
        change = scores[pl.ds(block, 2)].reshape(2 * HEAD, WIDE) * (wide_u[pl.ds(block, 2)].reshape(2 * HEAD, WIDE) - e)
        key = turned[:, pl.ds(pl.multiple_of(block * HEAD, HEAD), 2 * HEAD)]
        grad[...] += dot(key, change.astype(BF16))
        return 0

    lax.fori_loop(0, pairs, third, 0)
    est = functools.reduce(jnp.add, heads_of(e))
    mine = lax.broadcasted_iota(jnp.int32, est_ref.shape, 0) == row
    est_ref[...] = jnp.where(mine, est, est_in[...])
    max_ref[...] = top
    inv_ref[...] = inverse
    e_ref[...] = e
    out = grad[...] * (inverse * SCALE)
    for h, x in enumerate(heads_of(out)):
        g_out[:, h * HEAD : (h + 1) * HEAD] = x.T.astype(BF16)


def td_rows(own, others, rewards, starts, subset_ref, b, member):
    shape = (8, HEAD)
    rows = lax.broadcasted_iota(jnp.int32, shape, 0)
    lanes = lax.broadcasted_iota(jnp.int32, shape, 1)
    position = (rows * SIDE + b) * HEAD + lanes
    ahead = []
    for table, after in others:
        after = jnp.where(b == SIDE - 1, pltpu.roll(after, 7, 0), after)
        ahead.append(jnp.where(lanes == HEAD - 1, pltpu.roll(after, HEAD - 1, 1), pltpu.roll(table, HEAD - 1, 1)))
    lowest = None
    for k in range(subset_ref.shape[1]):
        apart = jnp.bitwise_xor(subset_ref[member, k], member)
        chosen = ahead[0]
        for i in range(1, MEMBERS):
            chosen = jnp.where(apart == i, ahead[i], chosen)
        lowest = chosen if lowest is None else jnp.minimum(lowest, chosen)
    goes_on = position + 1 < CHUNKS * HEAD
    for start in starts:
        goes_on = goes_on & (position + 1 != start)
    lowest = jnp.where(goes_on, lowest, 0.0)
    return own - (rewards + DISCOUNT * lowest)


def backward_kernel(*refs):
    q_parts, max_parts, inv_parts, e_parts, k_parts, refs = *(refs[4 * i : 4 * i + 4] for i in range(5)), refs[20:]
    (keys, us, rewards, start_ref, subset_ref), near, far, refs = refs[:5], *refs[5:7], refs[7:]
    td_own, d_outs, (stacked, turned, key_grad, sums, tds) = refs[0], refs[1:5], refs[5:]
    a, b = place()
    member = lax.rem(lax.axis_index("dp"), MEMBERS)
    starts = [start_ref[i] for i in range(TURNS - 1)]
    others = [(x[8 * i : 8 * i + 8], x[16 + 8 * i : 24 + 8 * i]) for x in (near, far) for i in range(2)]
    tds[...] = td_rows(near[:8], others, rewards[...], starts, subset_ref, b, member)
    td_own[...] = tds[pl.ds(a, 1), :]
    key_grad[...] = jnp.zeros_like(key_grad)
    sums[...] = jnp.zeros_like(sums)
    pick = selector(2 * GROUP)
    lanes = lax.broadcasted_iota(jnp.int32, (1, HEAD), 1)
    for s in range(SIDE):
        row = row_of(a, s)
        chunk = row * SIDE + b
        row_pos = chunk * HEAD + lanes
        row_start = latest(starts, row_pos)
        low = lax.div(latest(starts, chunk * HEAD), HEAD)
        stack_heads(q_parts[s], stacked)
        turn_heads(q_parts[s], turned)
        top, e = max_parts[s][...], e_parts[s][...]
        td = jnp.concatenate([tds[pl.ds(row, 1), :]] * GROUP, axis=1) * inv_parts[s][...]

        def one_pair(pair, _, low=low, row_pos=row_pos, row_start=row_start, top=top, e=e, td=td):
            block = low + 2 * pair
            score = dot(keys[pl.ds(block, 2)].reshape(2 * HEAD, HEAD), turned[...])
            seen = visible_at(block, row_pos, row_start, 2)
            prob = jnp.exp2((score - top) * (SCALE * LOG2E)) * td
            prob = jnp.concatenate([jnp.where(seen, x, 0.0) for x in heads_of(prob)], axis=1)
            u = jnp.concatenate([dot(us[block + i], pick, TN) for i in range(2)], axis=0)
            total = sums[pl.ds(block, 2)].reshape(2 * HEAD, HEAD)
            for h, part in enumerate(heads_of(prob)):
                total = total + jnp.where(lanes == h, jnp.sum(part, axis=1, keepdims=True), 0.0)
            sums[pl.ds(block, 2)] = total.reshape(2, HEAD, HEAD)
            out = dot((prob * (u - e)).astype(BF16), stacked[...])
            key_grad[pl.ds(block, 2)] += out.reshape(2, HEAD, HEAD)
            return 0

        lax.fori_loop(0, lax.div(chunk - low + 2, 2), one_pair, 0)
    heads = jnp.zeros((2 * GROUP, HEAD), F32)
    for t in range(SIDE):
        out = d_outs[(SIDE - t) % SIDE]
        for s in range(SIDE):
            chunk = ahead_by(a, -s) * SIDE + ahead_by(b, -t)
            high, low = split_two(sums[pl.ds(chunk, 1)][0].T[:GROUP])
            both = jnp.concatenate([high, low], axis=0).astype(BF16)
            heads = heads + dot(both, k_parts[t][s, HEAD + AUX :, :])
            base = s * GRAD_ROWS
            out[base : base + HEAD, :] = (key_grad[pl.ds(chunk, 1)][0] * SCALE).astype(BF16)
            out[base + HEAD : base + GRAD_ROWS, :] = both
    heads = heads[:GROUP] + heads[GROUP:]
    for t in range(SIDE):
        first = 2 * ahead_by(b, t)
        mine = pltpu.roll(heads, lax.rem(GROUP - first, GROUP), 0)
        d_outs[t][SIDE * GRAD_ROWS :, :] = jnp.concatenate(split_two(mine), axis=0).astype(BF16)


def collect_kernel(d0, d1, d2, d3, *outs):
    heads = [d[SIDE * GRAD_ROWS :, :].astype(F32) for d in (d0, d1, d2, d3)]
    outs[SIDE][...] = functools.reduce(jnp.add, [x[:GROUP] + x[GROUP:] for x in heads])
    for s in range(SIDE):
        base = s * GRAD_ROWS
        keys = [d[base : base + HEAD, :].astype(F32) for d in (d0, d1, d2, d3)]
        sums = [d[base + HEAD : base + GRAD_ROWS, :].astype(F32) for d in (d0, d1, d2, d3)]
        total = functools.reduce(jnp.add, [x[:GROUP] + x[GROUP:] for x in sums])
        outs[s][:HEAD, :] = functools.reduce(jnp.add, keys).astype(BF16)
        outs[s][HEAD:, :] = jnp.concatenate(split_two(total), axis=0).astype(BF16)


def finish_queries_kernel(td_ref, g0, g1, g2, g3, out):
    a, _ = place()
    td = jnp.broadcast_to(td_ref[...], (HEAD, HEAD)).T
    for s, part in enumerate((g0, g1, g2, g3)):
        base = ahead_by(a, s) * WIDE
        for h in range(GROUP):
            columns = pl.ds(pl.multiple_of(base + h * HEAD, HEAD), HEAD)
            block = part[:, h * HEAD : (h + 1) * HEAD].astype(F32)
            out[0, :, columns] = (block * td).astype(BF16)


def finish_keys_kernel(weight_ref, r0, r1, r2, r3, key_out, value_out):
    a, _ = place()
    member = lax.rem(lax.axis_index("dp"), MEMBERS)
    for s, part in enumerate((r0, r1, r2, r3)):
        group = ahead_by(a, s)
        columns = pl.ds(pl.multiple_of(group * HEAD, HEAD), HEAD)
        weights = group_weights(weight_ref, member, group)
        weights = jnp.concatenate([weights, weights], axis=0).astype(BF16)
        key_out[0, :, columns] = part[:HEAD, :]
        value_out[0, :, columns] = dot(part[HEAD:, :], weights, TN).astype(BF16)


def join_heads_kernel(h0, h1, h2, h3, out):
    member = lax.rem(lax.axis_index("dp"), MEMBERS)
    rows = lax.broadcasted_iota(jnp.int32, (2 * MEMBERS, HEAD), 0)
    total = jnp.zeros((2 * MEMBERS, HEAD), F32)
    for i, part in enumerate((h0, h1, h2, h3)):
        first = 2 * jnp.bitwise_xor(member, i)
        for j in range(2):
            total = jnp.where(rows == first + j, part[j : j + 1, :], total)
    out[...] = total


def finish_heads_kernel(half, other, out):
    total = half[...] + other[...]
    for m in range(MEMBERS):
        for j in range(2):
            out[m : m + 1, j * HEAD : (j + 1) * HEAD] = total[2 * m + j : 2 * m + j + 1, :]


def call(kernel, outs, operands, scratch=(), in_smem=(), out_smem=(), in_place=False, limit=16, us=1.0):
    def spec(i, smem):
        return pl.BlockSpec(memory_space=pltpu.SMEM if i in smem else pltpu.VMEM)

    in_specs = [pl.BlockSpec(memory_space=pltpu.HBM) if in_place else spec(i, in_smem) for i in range(len(operands))]

    return pl.pallas_call(
        kernel,
        out_shape=[jax.ShapeDtypeStruct(s, t) for s, t in outs],
        in_specs=in_specs,
        out_specs=[spec(i, out_smem) for i in range(len(outs))],
        scratch_shapes=list(scratch),
        compiler_params=pltpu.CompilerParams(vmem_limit_bytes=limit * 2**20),
        cost_estimate=pl.CostEstimate(flops=int(us * 1.1e9), bytes_accessed=0, transcendentals=0),
    )(*operands)


def per_device(queries, keys, values, segment_ids, rewards, value_weight, subset):
    tok = keys.shape[1]
    inputs = (queries, keys, values, segment_ids, rewards, value_weight)
    prepared = call(
        prepare_kernel,
        [((2 * tok + AUX, HEAD), BF16)] * SIDE + [((tok, WIDE), BF16)] * SIDE,
        inputs,
        [pltpu.VMEM(x.shape, x.dtype) for x in inputs[1:]] + [pltpu.SemaphoreType.DMA((len(inputs) - 1 + SIDE,))],
        in_place=True,
        limit=56,
    )
    key_own, q_own = prepared[:SIDE], prepared[SIDE:]
    key_msgs = [key_own[0]] + [along_x(key_own[s], s) for s in range(1, SIDE)]
    q_parts = [q_own[0]] + [along_x(q_own[s], s) for s in range(1, SIDE)]
    key_rows = jnp.stack(key_msgs)
    k_parts = [key_rows] + [along_y(key_rows, t) for t in range(1, SIDE)]
    by_chunk, turned, us, wide_u, reward_rows, starts = call(
        assemble_kernel,
        [
            ((CHUNKS + 1, HEAD, HEAD), BF16),
            ((HEAD, (CHUNKS + 1) * HEAD), BF16),
            ((CHUNKS + 1, 2 * GROUP, HEAD), BF16),
            ((CHUNKS + 1, HEAD, WIDE), F32),
            ((8, HEAD), F32),
            ((8,), jnp.int32),
        ],
        k_parts,
        out_smem=(5,),
        us=30.0,
    )
    by_chunk, q_parts = lax.optimization_barrier((by_chunk, q_parts))
    g_own, stats = [None] * SIDE, [None] * SIDE
    partial = jnp.zeros((8, HEAD), F32)
    for s in (0, 1, 3, 2):
        g_own[s], partial, *stats[s] = call(
            functools.partial(forward_kernel, s),
            [((tok, WIDE), BF16), ((8, HEAD), F32)] + [((1, WIDE), F32)] * 3,
            (q_parts[s], by_chunk, turned, wide_u, starts, partial),
            [
                pltpu.VMEM((HEAD, WIDE), BF16),
                pltpu.VMEM((CHUNKS + 1, HEAD, WIDE), F32),
                pltpu.VMEM((HEAD, WIDE), F32),
            ],
            in_smem=(4,),
            us=4.0,
        )
    est = partial + along_x(partial, 1) + along_x(partial, 2) + along_x(partial, 3)
    dp_count = lax.axis_size("dp")
    partner = {k: [(i, i ^ k) for i in range(dp_count)] for k in (1, 2, 3, 4, 8, 12)}
    est_pair = lax.ppermute(est, "dp", partner[1])
    after = along_y(est, -1)
    both = [
        (i, ((i // CHUNKS) ^ 1) * CHUNKS + i % CHUNKS // SIDE * SIDE + (i - 1) % SIDE)
        for i in range(dp_count * CHUNKS)
    ]
    after_pair = lax.ppermute(est, ("dp", "seq"), both)
    joined = jnp.concatenate([est, est_pair, after, after_pair])
    g_own, joined = lax.optimization_barrier((g_own, joined))
    far = lax.ppermute(joined, "dp", partner[2])
    g_parts = [g_own[0]] + [along_x(g_own[s], -s) for s in range(1, SIDE)]
    td_local, *grads = call(
        backward_kernel,
        [((1, tok), F32)] + [((SIDE * GRAD_ROWS + 2 * GROUP, HEAD), BF16)] * SIDE,
        (
            *q_parts,
            *(stats[s][i] for i in range(3) for s in range(SIDE)),
            *k_parts,
            *(by_chunk, us, reward_rows, starts, subset, joined, far),
        ),
        [
            pltpu.VMEM((WIDE, HEAD), BF16),
            pltpu.VMEM((HEAD, WIDE), BF16),
            pltpu.VMEM((CHUNKS + 1, HEAD, HEAD), F32),
            pltpu.VMEM((CHUNKS + 1, HEAD, HEAD), F32),
            pltpu.VMEM((8, HEAD), F32),
        ],
        in_smem=(23, 24),
        us=8.0,
    )
    td_local, g_parts = lax.optimization_barrier((td_local, g_parts))
    d_own = grads
    d_parts = [d_own[0]] + [along_y(d_own[t], t) for t in range(1, SIDE)]
    (query_grad,) = call(finish_queries_kernel, [(queries.shape, BF16)], (td_local, *g_parts), us=2.5)
    *d_parts, query_grad = lax.optimization_barrier((*d_parts, query_grad))
    *r_own, head_part = call(
        collect_kernel, [((GRAD_ROWS, HEAD), BF16)] * SIDE + [((GROUP, HEAD), F32)], d_parts
    )
    head_parts = [head_part] + [lax.ppermute(head_part, "dp", partner[k]) for k in range(1, MEMBERS)]
    (heads,) = call(join_heads_kernel, [((2 * MEMBERS, HEAD), F32)], head_parts)
    heads = heads + lax.ppermute(heads, "dp", partner[4])
    packs = [heads, lax.ppermute(heads, "dp", partner[8])]
    r_parts = [r_own[0]] + [along_x(r_own[s], -s) for s in range(1, SIDE)]
    key_grad, value_grad = call(
        finish_keys_kernel, [(keys.shape, BF16), (values.shape, BF16)], (value_weight, *r_parts)
    )
    (head_grad,) = call(finish_heads_kernel, [((MEMBERS, 2 * HEAD), F32)], packs)
    return query_grad, key_grad, value_grad, td_local, head_grad


def solution(mesh):
    return jax.shard_map(
        per_device,
        mesh=mesh,
        in_specs=(
            P("dp", "seq", None),
            P("dp", "seq", None),
            P("dp", "seq", None),
            P(None, "seq"),
            P(None, "seq"),
            P(),
            P(),
        ),
        out_specs=(
            P("dp", "seq", None),
            P("dp", "seq", None),
            P("dp", "seq", None),
            P("dp", "seq"),
            P(None, "seq"),
        ),
        check_vma=False,
    )
```
